32 devices in a mesh: fsdp: 4 (over y, core), ctx: 4 (over z), tp: 2 (over x).
Axes of the slice: x: 2, y: 2, z: 4, core: 2. Of those that a mesh axis runs over, the one named last changes fastest.
Arguments:
- tokens: bfloat16 [8, 2048, 960], P('fsdp', ('ctx', 'tp')), may hold values from -6 to 6
- cotangent: bfloat16 [8, 2048, 960], P('fsdp', ('ctx', 'tp')), may hold values from -6 to 6
- input_gain: bfloat16 [960], P('fsdp'), may hold values from 0.099609375 to 1.8984375
- w_query: bfloat16 [960, 960], P('fsdp'), may hold values from -0.1875 to 0.1875
- w_keyval: bfloat16 [960, 640], P('fsdp'), may hold values from -0.1875 to 0.1875
- w_output: bfloat16 [960, 960], P('fsdp'), may hold values from -2 to 2
- middle_gain: bfloat16 [960], P('fsdp'), may hold values from 0.099609375 to 1.8984375
- w_gate: bfloat16 [960, 2560], P('fsdp', 'tp'), may hold values from -0.1875 to 0.1875
- w_up: bfloat16 [960, 2560], P('fsdp', 'tp'), may hold values from -0.1875 to 0.1875
- w_down: bfloat16 [960, 2560], P('fsdp', 'tp'), may hold values from -0.25 to 0.25
Outputs:
- result: bfloat16 [8, 2048, 960], P('fsdp', ('ctx', 'tp'))
- grad_tokens: float32 [8, 2048, 960], P('fsdp', ('ctx', 'tp'))
- grad_input_gain: float32 [960], P('fsdp')
- grad_w_query: float32 [960, 960], P('fsdp')
- grad_w_keyval: float32 [960, 640], P('fsdp')
- grad_w_output: float32 [960, 960], P('fsdp')
- grad_middle_gain: float32 [960], P('fsdp')
- grad_w_gate: float32 [960, 2560], P('fsdp', 'tp')
- grad_w_up: float32 [960, 2560], P('fsdp', 'tp')
- grad_w_down: float32 [960, 2560], P('fsdp', 'tp')
The draws below stay inside these ranges and needn't reach their ends.
All inputs are finite; a program needn't handle non-finite values.
Results may differ from the reference program's by a relative error of at most 0.02.
Values may be sent and summed in bfloat16 or wider, within the bound.
A program may use at most 128 MiB of HBM per device.

```python
import jax
import jax.numpy as jnp
from jax import lax

D = 960
QUERY_HEADS = 15
KEYVAL_HEADS = 5
HEAD_WIDTH = 64
FF = 2560
SEQUENCE_LENGTH = 2048
QW = 960
KEY_WIDTH = 320
SEQS = 8


def with_spikes(array, stream_key, source, target, blocks, factor):
    def block_of(dim):
        return (jnp.arange(array.shape[dim]) // (array.shape[dim] // blocks)).reshape((-1,) + (1,) * (array.ndim - 1 - dim))

    near = jax.random.permutation(stream_key, blocks)[block_of(target)]
    far = (block_of(target) + blocks // 2) % blocks
    return jnp.where((block_of(source) == near) | (block_of(source) == far), factor * array, array)


def block_levels(stream_key, dims, split, low, largest):
    def one(position, parts):
        draws = jax.random.uniform(jax.random.fold_in(jax.random.fold_in(stream_key, 6), position), (parts,), jnp.float32, low / len(split), largest / len(split))
        return jnp.repeat(jnp.exp(draws), dims[position] // parts).reshape((-1,) + (1,) * (len(dims) - position - 1))

    loudness = one(*split[0])
    for cut in split[1:]:
        loudness = loudness * one(*cut)
    return loudness


def normal_values(key, extent, deviation, bound, pieces=(), held_as=jnp.bfloat16):
    array = jax.random.normal(key, extent, jnp.float32) * deviation
    if len(pieces) > 0:
        array = block_levels(key, extent, pieces, -0.22, 0.18) * array
    return jnp.clip(array, min=-bound, max=bound).astype(held_as)


def noise_with(stream_key, shape, scale, reach, shards, heavy, held_as=jnp.bfloat16):
    values = scale * jax.random.normal(stream_key, shape, jnp.float32)
    if shards:
        values = values * block_levels(stream_key, shape, shards, -0.22, 0.18)
    return jnp.clip(with_spikes(values, jax.random.fold_in(stream_key, 3), *heavy), -reach, reach).astype(held_as)


def setup_inputs(seed: int = 0) -> dict:
    key_list = jax.random.split(jax.random.key(seed), 11)
    tokens = noise_with(key_list[0], (SEQS, SEQUENCE_LENGTH, D), 1.0, 6.0, ((0, 4), (1, 8)), (0, 2, 4, 2.0))
    cotangent = noise_with(key_list[1], (SEQS, SEQUENCE_LENGTH, D), 1.0, 6.0, ((0, 4), (1, 8)), (0, 2, 4, 2.0))
    input_gain = jnp.clip(1.0 + 0.18 * jax.random.normal(key_list[2], (D,), jnp.float32), 0.099609375, 1.8984375).astype(jnp.bfloat16)
    w_query = normal_values(key_list[3], (D, QW), D ** -0.5, 0.1875, ((0, 4),))
    w_keyval = normal_values(key_list[4], (D, 2 * KEY_WIDTH), D ** -0.5, 0.1875, ((0, 4),))
    w_output = normal_values(key_list[5], (QW, D), (max(1, QW * 16 // SEQUENCE_LENGTH)) ** -0.5, 2.0, ((0, 4),))
    middle_gain = jnp.clip(1.0 + 0.18 * jax.random.normal(key_list[6], (D,), jnp.float32), 0.099609375, 1.8984375).astype(jnp.bfloat16)
    w_gate = normal_values(key_list[7], (D, FF), D ** -0.5, 0.1875, ((0, 4), (1, 2)))
    w_up = normal_values(key_list[8], (D, FF), D ** -0.5, 0.1875, ((0, 4), (1, 2)))
    w_down = normal_values(key_list[9], (D, FF), (FF // 4) ** -0.5, 0.25, ((0, 4), (1, 2)))
    return {"tokens": tokens, "cotangent": cotangent, "input_gain": input_gain, "w_query": w_query, "w_keyval": w_keyval, "w_output": w_output, "middle_gain": middle_gain, "w_gate": w_gate, "w_up": w_up, "w_down": w_down}


EPS = 1e-05
THETA = 10000.0
precise = lax.Precision.HIGHEST

@jax.custom_vjp
def reduced_precision(v):
    return lax.optimization_barrier(v.astype(jnp.bfloat16)).astype(jnp.float32)

@jax.custom_vjp
def low_back(v):
    return v

def low_keep(v):
    return (reduced_precision(v), None)

def low_pass(kept, grad):
    return (grad,)

def back_keep(v):
    return (v, None)

def back_low(kept, grad):
    return (reduced_precision(grad),)
reduced_precision.defvjp(low_keep, low_pass)
low_back.defvjp(back_keep, back_low)

def normalize(value_rows):
    return value_rows * lax.rsqrt(lax.optimization_barrier(jnp.mean(value_rows * value_rows, -1, keepdims=True)) + EPS)

def apply_rotary(value_rows, cosine_table, sine_table, heads):
    half_width = HEAD_WIDTH // 2
    shaped = value_rows.reshape(value_rows.shape[:-1] + (heads, HEAD_WIDTH))
    leading = shaped[..., :half_width]
    trailing = shaped[..., half_width:]
    cosine_wide = cosine_table[:, None, :]
    sine_wide = sine_table[:, None, :]
    turned = jnp.concatenate([leading * cosine_wide - trailing * sine_wide, trailing * cosine_wide + leading * sine_wide], -1)
    return turned.reshape(value_rows.shape)

def attend(head_items):
    query_rotated, key_rotated, value_reduced = head_items
    group_total = QUERY_HEADS // KEYVAL_HEADS
    query_by_group = query_rotated.reshape(SEQUENCE_LENGTH, KEYVAL_HEADS, group_total, HEAD_WIDTH)
    key_by_group = key_rotated.reshape(SEQUENCE_LENGTH, KEYVAL_HEADS, HEAD_WIDTH)
    value_by_group = value_reduced.reshape(SEQUENCE_LENGTH, KEYVAL_HEADS, HEAD_WIDTH)
    scores = jnp.einsum('qjgd,kjd->jgqk', query_by_group, key_by_group, precision=precise) * HEAD_WIDTH ** (-0.5)
    scores = low_back(scores)
    allowed = jnp.arange(SEQUENCE_LENGTH)[None, :] <= jnp.arange(SEQUENCE_LENGTH)[:, None]
    weights = jax.nn.softmax(jnp.where(allowed, scores, -jnp.inf), axis=-1)
    mixed_heads = jnp.einsum('jgqk,kjd->qjgd', reduced_precision(weights), value_by_group, precision=precise)
    return mixed_heads.reshape(SEQUENCE_LENGTH, QUERY_HEADS * HEAD_WIDTH)

def layer_forward(inputs, weights, cosine_table, sine_table):
    input_gain, w_query, w_keyval, w_output, middle_gain, w_gate, w_up, w_down = weights
    normed_one = reduced_precision(normalize(inputs) * input_gain)
    query_raw = low_back(jnp.dot(normed_one, w_query, precision=precise))
    keyval_unrotated = low_back(jnp.dot(normed_one, w_keyval, precision=precise))
    query_rotated = reduced_precision(apply_rotary(query_raw, cosine_table, sine_table, QUERY_HEADS))
    key_rotated = reduced_precision(apply_rotary(keyval_unrotated[..., :KEY_WIDTH], cosine_table, sine_table, KEYVAL_HEADS))
    value_reduced = reduced_precision(keyval_unrotated[..., KEY_WIDTH:])
    mixed_all = lax.map(jax.checkpoint(attend), (query_rotated, key_rotated, value_reduced))
    mixed_low = reduced_precision(low_back(mixed_all))
    attention_out = low_back(jnp.dot(mixed_low, w_output, precision=precise))
    middle = inputs + attention_out
    normed_two = reduced_precision(normalize(middle) * middle_gain)
    gate_proj = low_back(jnp.dot(normed_two, w_gate, precision=precise))
    up_proj = low_back(jnp.dot(normed_two, w_up, precision=precise))
    hidden = reduced_precision(jax.nn.silu(gate_proj) * up_proj)
    feed_out = low_back(jnp.einsum('bsf,df->bsd', hidden, w_down, precision=precise))
    return middle + feed_out

def reference(tokens, cotangent, input_gain, w_query, w_keyval, w_output, middle_gain, w_gate, w_up, w_down):
    params = tuple((weight.astype(jnp.float32) for weight in (input_gain, w_query, w_keyval, w_output, middle_gain, w_gate, w_up, w_down)))
    half_width = HEAD_WIDTH // 2
    positions = jnp.arange(SEQUENCE_LENGTH).astype(jnp.float32)
    frequency = THETA ** (-(2.0 * jnp.arange(half_width).astype(jnp.float32)) / HEAD_WIDTH)
    angles = positions[:, None] * frequency[None, :]
    cosine_table = jnp.cos(angles)
    sine_table = jnp.sin(angles)
    group_size = 2 if SEQS % 2 == 0 else 1
    group_count = SEQS // group_size
    token_groups = tokens.reshape(group_count, group_size, SEQUENCE_LENGTH, D)
    cotangent_groups = cotangent.reshape(group_count, group_size, SEQUENCE_LENGTH, D)

    def forward(inputs, weights):
        return layer_forward(inputs, weights, cosine_table, sine_table)

    def group_step(totals, group_items):
        inputs = group_items[0].astype(jnp.float32)
        outputs, pullback = jax.vjp(forward, inputs, params)
        back_inputs, back_weights = pullback(group_items[1].astype(jnp.float32))
        totals = jax.tree.map(jnp.add, totals, back_weights)
        return (totals, (outputs.astype(jnp.bfloat16), back_inputs))
    zeros_start = tuple((jnp.zeros_like(weight) for weight in params))
    totals, (results, back_tokens) = lax.scan(group_step, zeros_start, (token_groups, cotangent_groups))
    return (results.reshape(SEQS, SEQUENCE_LENGTH, D), back_tokens.reshape(SEQS, SEQUENCE_LENGTH, D), totals[0], totals[1], totals[2], totals[3], totals[4], totals[5], totals[6], totals[7])
```

```python
import jax
import jax.numpy as jnp
from jax import lax
from jax.experimental import pallas as pl
from jax.experimental.pallas import tpu as pltpu
from jax.sharding import PartitionSpec as P

QUERY_HEADS = 15
KEYVAL_HEADS = 5
GROUP = QUERY_HEADS // KEYVAL_HEADS
HEAD_WIDTH = 64
HALF = HEAD_WIDTH // 2
KEY_WIDTH = 320
QUERY_WIDTH = QUERY_HEADS * HEAD_WIDTH
SCALE = HEAD_WIDTH ** (-0.5)

EPS = 1e-05
THETA = 10000.0
VMEM_LIMIT = 40 * 1024 * 1024


def dot(left, right, left_dim, right_dim):
    return lax.dot_general(
        left, right, (((left_dim,), (right_dim,)), ((), ())), preferred_element_type=jnp.float32
    )


def rope_tables(token_positions, first_place):
    position = (first_place + lax.iota(jnp.int32, token_positions)).astype(jnp.float32)
    frequency = THETA ** (-(2.0 * lax.iota(jnp.int32, HALF).astype(jnp.float32)) / HEAD_WIDTH)
    angles = frequency[:, None] * position[None, :]
    return (jnp.cos(angles), jnp.sin(angles))


def apply_rotary(rows, cosine, sine):
    shaped = rows.reshape(-1, 2, HALF, rows.shape[-1])
    leading = shaped[:, 0]
    trailing = shaped[:, 1]
    return jnp.stack(
        [leading * cosine - trailing * sine, trailing * cosine + leading * sine], 1
    ).reshape(rows.shape)


def normalize(value_rows):
    inverse_rms = lax.rsqrt(jnp.mean(value_rows * value_rows, -1, keepdims=True) + EPS)
    return (value_rows * inverse_rms, inverse_rms)


def norm_back(back_unit, unit_rows, inverse_rms):
    return inverse_rms * (
        back_unit - unit_rows * jnp.mean(back_unit * unit_rows, -1, keepdims=True)
    )


def causal(scores):
    key_place = lax.broadcasted_iota(jnp.int32, scores.shape, 0)
    query_place = lax.broadcasted_iota(jnp.int32, scores.shape, 1)
    return jnp.where(key_place <= query_place, scores, -jnp.inf)


def forward_kernel(query_ref, key_ref, value_ref, mixed_ref, lse_ref):
    place = lax.axis_index("ctx")
    queries = [query_ref[g] * jnp.bfloat16(SCALE) for g in range(GROUP)]

    def scores_of(keys_turned, g, masked):
        scores = dot(keys_turned, queries[g], 1, 0)
        return causal(scores) if masked else scores

    def first():
        keys_turned = key_ref[place, 0, 0].T
        values = value_ref[place, 0, 0]
        carried = []
        for g in range(GROUP):
            scores = scores_of(keys_turned, g, True)
            top = jnp.max(scores, 0, keepdims=True)
            lifted = jnp.exp(scores - top)
            total = jnp.sum(lifted, 0, keepdims=True)
            carried += [top, total, dot(values, lifted.astype(jnp.bfloat16), 1, 0)]
        return tuple(carried)

    def step(block, carried):
        keys_turned = key_ref[block, 0, 0].T
        values = value_ref[block, 0, 0]
        later = []
        for g in range(GROUP):
            top, total, mixed = carried[3 * g : 3 * g + 3]
            scores = scores_of(keys_turned, g, False)
            new_top = jnp.maximum(top, jnp.max(scores, 0, keepdims=True))
            lifted = jnp.exp(scores - new_top)
            shrink = jnp.exp(top - new_top)
            later += [
                new_top,
                total * shrink + jnp.sum(lifted, 0, keepdims=True),
                mixed * shrink + dot(values, lifted.astype(jnp.bfloat16), 1, 0),
            ]
        return tuple(later)

    carried = lax.fori_loop(0, place, step, first())
    for g in range(GROUP):
        top, total, mixed = carried[3 * g : 3 * g + 3]
        mixed_ref[g] = (mixed / total).astype(jnp.bfloat16)
        lse_ref[g] = top + jnp.log(total)


def attend_forward(query, keyval):
    blocks, token_positions = keyval.shape[0], keyval.shape[-1]
    head_block = (GROUP, HEAD_WIDTH, token_positions)
    key_block = (blocks, 1, 1, HEAD_WIDTH, token_positions)
    area = QUERY_HEADS * token_positions * token_positions * blocks
    return pl.pallas_call(
        forward_kernel,
        grid=(KEYVAL_HEADS,),
        in_specs=[
            pl.BlockSpec(head_block, lambda j: (j, 0, 0)),
            pl.BlockSpec(key_block, lambda j: (0, 0, j, 0, 0)),
            pl.BlockSpec(key_block, lambda j: (0, 1, j, 0, 0)),
        ],
        out_specs=[
            pl.BlockSpec(head_block, lambda j: (j, 0, 0)),
            pl.BlockSpec((GROUP, 1, token_positions), lambda j: (j, 0, 0)),
        ],
        out_shape=[
            jax.ShapeDtypeStruct(query.shape, jnp.bfloat16),
            jax.ShapeDtypeStruct((QUERY_HEADS, 1, token_positions), jnp.float32),
        ],
        compiler_params=pltpu.CompilerParams(vmem_limit_bytes=VMEM_LIMIT),
        cost_estimate=pl.CostEstimate(
            flops=16 * HEAD_WIDTH * area, bytes_accessed=6 * query.size, transcendentals=area
        ),
        name="attend_forward",
    )(query, keyval, keyval)


def backward_kernel(
    query_ref, key_ref, value_ref, back_ref, mixed_ref, lse_ref, cosine_ref, sine_ref,
    back_query_ref, back_keyval_ref,
):
    place = lax.axis_index("ctx")
    blocks = key_ref.shape[0]
    queries = [query_ref[g] * jnp.bfloat16(SCALE) for g in range(GROUP)]
    backs = [back_ref[g] for g in range(GROUP)]
    tops = [lse_ref[g] for g in range(GROUP)]
    sums = [
        jnp.sum(backs[g].astype(jnp.float32) * mixed_ref[g].astype(jnp.float32), 0, keepdims=True)
        for g in range(GROUP)
    ]

    def step(block, carried, masked=False):
        keys = key_ref[block, 0, 0]
        keys_turned = keys.T
        values_turned = value_ref[block, 0, 0].T
        back_key = jnp.zeros(keys.shape, jnp.float32)
        back_value = jnp.zeros(keys.shape, jnp.float32)
        later = []
        for g in range(GROUP):
            scores = dot(keys_turned, queries[g], 1, 0)
            if masked:
                scores = causal(scores)
            weights = jnp.exp(scores - tops[g])
            back_weights = dot(values_turned, backs[g], 1, 0)
            back_scores = (weights * (back_weights - sums[g])).astype(jnp.bfloat16)
            later.append(carried[g] + dot(keys, back_scores, 1, 0))
            back_key += dot(queries[g], back_scores, 1, 1)
            back_value += dot(backs[g], weights.astype(jnp.bfloat16), 1, 1)
        back_keyval_ref[block, 0, 0] = back_key.astype(jnp.bfloat16)
        back_keyval_ref[block, 1, 0] = back_value.astype(jnp.bfloat16)
        return tuple(later)

    start = tuple(jnp.zeros(query_ref.shape[1:], jnp.float32) for g in range(GROUP))
    carried = lax.fori_loop(0, place, step, step(place, start, True))

    def clear(block, unused):
        zero = jnp.zeros(key_ref.shape[3:], jnp.bfloat16)
        back_keyval_ref[block, 0, 0] = zero
        back_keyval_ref[block, 1, 0] = zero
        return unused

    lax.fori_loop(place + 1, blocks, clear, 0)
    cosine = cosine_ref[...]
    sine = sine_ref[...]
    for g in range(GROUP):
        leading = carried[g][:HALF] * SCALE
        trailing = carried[g][HALF:] * SCALE
        back_query_ref[g, :HALF] = (leading * cosine + trailing * sine).astype(jnp.bfloat16)
        back_query_ref[g, HALF:] = (trailing * cosine - leading * sine).astype(jnp.bfloat16)


def attend_backward(query, keyval, back_mixed, mixed, lse, cosine, sine, first, count):
    blocks, token_positions = keyval.shape[0], keyval.shape[-1]
    head_block = (GROUP, HEAD_WIDTH, token_positions)
    key_block = (blocks, 1, 1, HEAD_WIDTH, token_positions)
    area = count * GROUP * token_positions * token_positions * blocks
    heads = pl.BlockSpec(head_block, lambda j: (j + first, 0, 0))
    table = pl.BlockSpec((HALF, token_positions), lambda j: (0, 0))
    return pl.pallas_call(
        backward_kernel,
        grid=(count,),
        in_specs=[
            heads,
            pl.BlockSpec(key_block, lambda j: (0, 0, j + first, 0, 0)),
            pl.BlockSpec(key_block, lambda j: (0, 1, j + first, 0, 0)),
            heads,
            heads,
            pl.BlockSpec((GROUP, 1, token_positions), lambda j: (j + first, 0, 0)),
            table,
            table,
        ],
        out_specs=[
            pl.BlockSpec(head_block, lambda j: (j, 0, 0)),
            pl.BlockSpec((blocks, 2, 1, HEAD_WIDTH, token_positions), lambda j: (0, 0, j, 0, 0)),
        ],
        out_shape=[
            jax.ShapeDtypeStruct((count * GROUP, HEAD_WIDTH, token_positions), jnp.bfloat16),
            jax.ShapeDtypeStruct(
                (blocks, 2, count, HEAD_WIDTH, token_positions), jnp.bfloat16
            ),
        ],
        compiler_params=pltpu.CompilerParams(vmem_limit_bytes=VMEM_LIMIT),
        cost_estimate=pl.CostEstimate(
            flops=40 * HEAD_WIDTH * area, bytes_accessed=10 * query.size, transcendentals=area
        ),
        name="attend_backward",
    )(query, keyval, keyval, back_mixed, mixed, lse, cosine, sine)


def on_device(
    tokens, cotangent, input_gain, w_query, w_keyval, w_output, middle_gain, w_gate, w_up, w_down
):
    half = lax.axis_index("tp")
    low_half = half == 0
    pair = [(0, 1), (1, 0)]

    def to_partner(value_rows):
        return lax.ppermute(value_rows, "tp", pair)

    def in_order(mine, received):
        return jnp.concatenate(
            [jnp.where(low_half, mine, received), jnp.where(low_half, received, mine)], 0
        )

    def take(value_rows, index):
        return lax.dynamic_index_in_dim(value_rows, index, 0, keepdims=False)

    tokens_own = in_order(take(tokens, half), to_partner(take(tokens, 1 - half)))
    full_gain_one, full_gain_two = (
        lax.all_gather(input_gain, "fsdp", axis=0, tiled=True),
        lax.all_gather(middle_gain, "fsdp", axis=0, tiled=True),
    )
    full_in = lax.all_gather(jnp.concatenate([w_query, w_keyval], 1), "fsdp", axis=0, tiled=True)
    full_output = lax.all_gather(w_output, "fsdp", axis=0, tiled=True)
    full_gate = lax.all_gather(w_gate, "fsdp", axis=0, tiled=True)
    full_up = lax.all_gather(w_up, "fsdp", axis=0, tiled=True)
    full_down = lax.all_gather(w_down, "fsdp", axis=0, tiled=True)
    cotangent_received = to_partner(cotangent)
    cotangent_own = in_order(take(cotangent, half), take(cotangent_received, half))
    cotangent_other = in_order(take(cotangent, 1 - half), take(cotangent_received, 1 - half))

    token_positions = tokens_own.shape[0]
    cosine, sine = rope_tables(token_positions, lax.axis_index("ctx") * token_positions)
    gain_one = full_gain_one.astype(jnp.float32)
    inputs = tokens_own.astype(jnp.float32)
    unit_one, inverse_one = normalize(inputs)
    normed_one = (unit_one * gain_one).astype(jnp.bfloat16)
    keyval_raw = dot(full_in[:, QUERY_WIDTH:], normed_one, 0, 1)
    keyval_low = jnp.concatenate(
        [apply_rotary(keyval_raw[:KEY_WIDTH], cosine, sine), keyval_raw[KEY_WIDTH:]], 0
    ).astype(jnp.bfloat16)
    keyval = lax.all_gather(keyval_low, "ctx", axis=0, tiled=False)
    keyval = keyval.reshape(keyval.shape[0], 2, KEYVAL_HEADS, HEAD_WIDTH, token_positions)
    query_raw = dot(full_in[:, :QUERY_WIDTH], normed_one, 0, 1)
    query_low = (
        apply_rotary(query_raw, cosine, sine)
        .astype(jnp.bfloat16)
        .reshape(QUERY_HEADS, HEAD_WIDTH, token_positions)
    )
    mixed_heads, lse = attend_forward(query_low, keyval)
    mixed_low = mixed_heads.reshape(QUERY_WIDTH, token_positions)
    middle = inputs + dot(mixed_low, full_output, 0, 0)

    gain_two = full_gain_two.astype(jnp.float32)
    unit_two, inverse_two = normalize(middle)
    normed_two = (unit_two * gain_two).astype(jnp.bfloat16)
    normed_other = to_partner(normed_two)

    def feed(rows, back_rows):
        gate_proj = dot(rows, full_gate, 1, 0)
        up_proj = dot(rows, full_up, 1, 0)
        sigmoid_gate = jax.nn.sigmoid(gate_proj)
        swish_gate = gate_proj * sigmoid_gate
        hidden = (swish_gate * up_proj).astype(jnp.bfloat16)
        back_hidden = dot(back_rows, full_down, 1, 0)
        back_gate = (
            back_hidden * up_proj * sigmoid_gate * (1.0 + gate_proj * (1.0 - sigmoid_gate))
        ).astype(jnp.bfloat16)
        back_up = (back_hidden * swish_gate).astype(jnp.bfloat16)
        return (hidden, back_gate, back_up)

    def feed_input_back(back_gate, back_up):
        return dot(back_gate, full_gate, 1, 1) + dot(back_up, full_up, 1, 1)

    hidden_own, back_gate_own, back_up_own = feed(normed_two, cotangent_own)
    hidden_other, back_gate_other, back_up_other = feed(normed_other, cotangent_other)
    back_two_received = to_partner(
        feed_input_back(back_gate_other, back_up_other).astype(jnp.bfloat16)
    )
    back_two = feed_input_back(back_gate_own, back_up_own) + back_two_received.astype(jnp.float32)
    feed_received = to_partner(dot(hidden_other, full_down, 1, 1).astype(jnp.bfloat16))
    result_own = (
        middle + dot(hidden_own, full_down, 1, 1) + feed_received.astype(jnp.float32)
    ).astype(jnp.bfloat16)

    def feed_gradient(left_own, right_own, left_other, right_other):
        gradient = dot(left_own, right_own, 0, 0) + dot(left_other, right_other, 0, 0)
        shared = lax.psum_scatter(
            gradient.astype(jnp.bfloat16), "fsdp", scatter_dimension=0, tiled=True
        )
        return lax.psum(shared, "ctx").astype(jnp.float32)

    share_down = feed_gradient(cotangent_own, hidden_own, cotangent_other, hidden_other)
    share_gate = feed_gradient(normed_two, back_gate_own, normed_other, back_gate_other)
    share_up = feed_gradient(normed_two, back_up_own, normed_other, back_up_other)

    grad_gain_two = jnp.sum(back_two * unit_two, axis=0)
    back_middle = cotangent_own.astype(jnp.float32) + norm_back(
        back_two * gain_two, unit_two, inverse_two
    )
    back_attention = back_middle.astype(jnp.bfloat16)
    back_mixed = dot(full_output, back_attention, 1, 1).astype(jnp.bfloat16)
    back_mixed = back_mixed.reshape(query_low.shape)
    grad_output = dot(mixed_low, back_attention, 1, 0).astype(jnp.bfloat16)
    share_output = lax.psum(
        lax.psum_scatter(grad_output, "fsdp", scatter_dimension=0, tiled=True), ("ctx", "tp")
    ).astype(jnp.float32)

    back_query = []
    back_key = []
    back_value = []
    for first, count in ((0, 3), (3, 2)):
        part_query, part_keyval = attend_backward(
            query_low, keyval, back_mixed, mixed_heads, lse, cosine, sine, first, count
        )
        owned = lax.psum_scatter(
            part_keyval.reshape(keyval.shape[0], 2 * count * HEAD_WIDTH, token_positions),
            "ctx",
            scatter_dimension=0,
            tiled=False,
        ).astype(jnp.float32)
        back_query.append(part_query.reshape(-1, token_positions))
        back_key.append(
            apply_rotary(owned[: count * HEAD_WIDTH], cosine, -sine).astype(jnp.bfloat16)
        )
        back_value.append(owned[count * HEAD_WIDTH :].astype(jnp.bfloat16))
    back_in = jnp.concatenate(back_query + back_key + back_value, 0)
    grad_in = dot(normed_one, back_in, 0, 1)
    back_one = dot(back_in, full_in, 0, 1)
    grad_gain_one = jnp.sum(back_one * unit_one, axis=0)
    back_inputs = back_middle + norm_back(back_one * gain_one, unit_one, inverse_one)

    def to_positions(value_rows):
        split = value_rows.reshape(2, token_positions // 2, value_rows.shape[-1])
        received = to_partner(take(split, 1 - half))
        return in_order(take(split, half)[None], received[None])

    result = to_positions(result_own)
    grad_tokens = to_positions(back_inputs.astype(jnp.bfloat16)).astype(jnp.float32)
    gradients = jnp.concatenate([grad_in, grad_gain_one[:, None], grad_gain_two[:, None]], 1)
    share_in = lax.psum(
        lax.psum_scatter(
            gradients.astype(jnp.bfloat16), "fsdp", scatter_dimension=0, tiled=True
        ),
        ("ctx", "tp"),
    ).astype(jnp.float32)
    width = full_in.shape[1]
    return (
        result,
        grad_tokens,
        share_in[:, width],
        share_in[:, :QUERY_WIDTH],
        share_in[:, QUERY_WIDTH:width],
        share_output,
        share_in[:, width + 1],
        share_gate,
        share_up,
        share_down,
    )


def solution(mesh):
    rows = P("fsdp", ("ctx", "tp"), None)
    specs = (
        P("fsdp"), P("fsdp", None), P("fsdp", None), P("fsdp", None),
        P("fsdp"), P("fsdp", "tp"), P("fsdp", "tp"), P("fsdp", "tp"),
    )
    return jax.shard_map(
        on_device,
        mesh=mesh,
        in_specs=(rows, rows) + specs,
        out_specs=(rows, rows) + specs,
        check_vma=False,
    )
```

```python
import jax
import jax.numpy as jnp
from jax import lax
from jax.experimental import pallas as pl
from jax.experimental.pallas import tpu as pltpu
from jax.sharding import PartitionSpec as P

QUERY_HEADS = 15
KEYVAL_HEADS = 5
GROUP = QUERY_HEADS // KEYVAL_HEADS
HEAD_WIDTH = 64
HALF = HEAD_WIDTH // 2
KEY_WIDTH = 320
QUERY_WIDTH = QUERY_HEADS * HEAD_WIDTH
SCALE = HEAD_WIDTH ** (-0.5)

EPS = 1e-05
THETA = 10000.0
VMEM_LIMIT = 40 * 1024 * 1024


def dot(left, right, left_dim, right_dim):
    return lax.dot_general(
        left, right, (((left_dim,), (right_dim,)), ((), ())), preferred_element_type=jnp.float32
    )


def rope_tables(token_positions, first_place):
    position = (first_place + lax.iota(jnp.int32, token_positions)).astype(jnp.float32)
    frequency = THETA ** (-(2.0 * lax.iota(jnp.int32, HALF).astype(jnp.float32)) / HEAD_WIDTH)
    angles = frequency[:, None] * position[None, :]
    return (jnp.cos(angles), jnp.sin(angles))


def apply_rotary(rows, cosine, sine):
    shaped = rows.reshape(-1, 2, HALF, rows.shape[-1])
    leading = shaped[:, 0]
    trailing = shaped[:, 1]
    return jnp.stack(
        [leading * cosine - trailing * sine, trailing * cosine + leading * sine], 1
    ).reshape(rows.shape)


def normalize(value_rows):
    inverse_rms = lax.rsqrt(jnp.mean(value_rows * value_rows, -1, keepdims=True) + EPS)
    return (value_rows * inverse_rms, inverse_rms)


def norm_back(back_unit, unit_rows, inverse_rms):
    return inverse_rms * (
        back_unit - unit_rows * jnp.mean(back_unit * unit_rows, -1, keepdims=True)
    )


def causal(scores):
    key_place = lax.broadcasted_iota(jnp.int32, scores.shape, 0)
    query_place = lax.broadcasted_iota(jnp.int32, scores.shape, 1)
    return jnp.where(key_place <= query_place, scores, -jnp.inf)


def forward_kernel(query_ref, key_ref, value_ref, mixed_ref, lse_ref):
    place = lax.axis_index("ctx")
    queries = [query_ref[g] * jnp.bfloat16(SCALE) for g in range(GROUP)]

    def scores_of(keys_turned, g, masked):
        scores = dot(keys_turned, queries[g], 1, 0)
        return causal(scores) if masked else scores

    def first():
        keys_turned = key_ref[0, 0, 0].T
        values = value_ref[0, 0, 0]
        carried = []
        for g in range(GROUP):
            scores = scores_of(keys_turned, g, True)
            top = jnp.max(scores, 0, keepdims=True)
            lifted = jnp.exp(scores - top)
            total = jnp.sum(lifted, 0, keepdims=True)
            carried += [top, total, dot(values, lifted.astype(jnp.bfloat16), 1, 0)]
        return tuple(carried)

    def step(block, carried):
        keys_turned = key_ref[block, 0, 0].T
        values = value_ref[block, 0, 0]
        later = []
        for g in range(GROUP):
            top, total, mixed = carried[3 * g : 3 * g + 3]
            scores = scores_of(keys_turned, g, False)
            new_top = jnp.maximum(top, jnp.max(scores, 0, keepdims=True))
            lifted = jnp.exp(scores - new_top)
            shrink = jnp.exp(top - new_top)
            later += [
                new_top,
                total * shrink + jnp.sum(lifted, 0, keepdims=True),
                mixed * shrink + dot(values, lifted.astype(jnp.bfloat16), 1, 0),
            ]
        return tuple(later)

    carried = lax.fori_loop(1, place + 1, step, first())
    for g in range(GROUP):
        top, total, mixed = carried[3 * g : 3 * g + 3]
        mixed_ref[g] = (mixed / total).astype(jnp.bfloat16)
        lse_ref[g] = top + jnp.log(total)


def attend_forward(query, keyval):
    blocks, token_positions = keyval.shape[0], keyval.shape[-1]
    head_block = (GROUP, HEAD_WIDTH, token_positions)
    key_block = (blocks, 1, 1, HEAD_WIDTH, token_positions)
    area = QUERY_HEADS * token_positions * token_positions * blocks
    return pl.pallas_call(
        forward_kernel,
        grid=(KEYVAL_HEADS,),
        in_specs=[
            pl.BlockSpec(head_block, lambda j: (j, 0, 0)),
            pl.BlockSpec(key_block, lambda j: (0, 0, j, 0, 0)),
            pl.BlockSpec(key_block, lambda j: (0, 1, j, 0, 0)),
        ],
        out_specs=[
            pl.BlockSpec(head_block, lambda j: (j, 0, 0)),
            pl.BlockSpec((GROUP, 1, token_positions), lambda j: (j, 0, 0)),
        ],
        out_shape=[
            jax.ShapeDtypeStruct(query.shape, jnp.bfloat16),
            jax.ShapeDtypeStruct((QUERY_HEADS, 1, token_positions), jnp.float32),
        ],
        compiler_params=pltpu.CompilerParams(vmem_limit_bytes=VMEM_LIMIT),
        cost_estimate=pl.CostEstimate(
            flops=16 * HEAD_WIDTH * area, bytes_accessed=6 * query.size, transcendentals=area
        ),
        name="attend_forward",
    )(query, keyval, keyval)


def backward_kernel(
    query_ref, key_ref, value_ref, back_ref, mixed_ref, lse_ref, cosine_ref, sine_ref,
    back_query_ref, back_keyval_ref,
):
    place = lax.axis_index("ctx")
    blocks = key_ref.shape[0]
    queries = [query_ref[g] * jnp.bfloat16(SCALE) for g in range(GROUP)]
    backs = [back_ref[g] for g in range(GROUP)]
    tops = [lse_ref[g] for g in range(GROUP)]
    sums = [
        jnp.sum(backs[g].astype(jnp.float32) * mixed_ref[g].astype(jnp.float32), 0, keepdims=True)
        for g in range(GROUP)
    ]

    def step(block, carried, masked=False):
        keys = key_ref[block, 0, 0]
        keys_turned = keys.T
        values_turned = value_ref[block, 0, 0].T
        back_key = jnp.zeros(keys.shape, jnp.float32)
        back_value = jnp.zeros(keys.shape, jnp.float32)
        later = []
        for g in range(GROUP):
            scores = dot(keys_turned, queries[g], 1, 0)
            if masked:
                scores = causal(scores)
            weights = jnp.exp(scores - tops[g])
            back_weights = dot(values_turned, backs[g], 1, 0)
            back_scores = (weights * (back_weights - sums[g])).astype(jnp.bfloat16)
            later.append(carried[g] + dot(keys, back_scores, 1, 0))
            back_key += dot(queries[g], back_scores, 1, 1)
            back_value += dot(backs[g], weights.astype(jnp.bfloat16), 1, 1)
        back_keyval_ref[block, 0, 0] = back_key.astype(jnp.bfloat16)
        back_keyval_ref[block, 1, 0] = back_value.astype(jnp.bfloat16)
        return tuple(later)

    start = tuple(jnp.zeros(query_ref.shape[1:], jnp.float32) for g in range(GROUP))
    carried = lax.fori_loop(1, place + 1, step, step(0, start, True))

    def clear(block, unused):
        zero = jnp.zeros(key_ref.shape[3:], jnp.bfloat16)
        back_keyval_ref[block, 0, 0] = zero
        back_keyval_ref[block, 1, 0] = zero
        return unused

    lax.fori_loop(place + 1, blocks, clear, 0)
    cosine = cosine_ref[...]
    sine = sine_ref[...]
    for g in range(GROUP):
        leading = carried[g][:HALF] * SCALE
        trailing = carried[g][HALF:] * SCALE
        back_query_ref[g, :HALF] = (leading * cosine + trailing * sine).astype(jnp.bfloat16)
        back_query_ref[g, HALF:] = (trailing * cosine - leading * sine).astype(jnp.bfloat16)


def attend_backward(query, keyval, back_mixed, mixed, lse, cosine, sine, first, count):
    blocks, token_positions = keyval.shape[0], keyval.shape[-1]
    head_block = (GROUP, HEAD_WIDTH, token_positions)
    key_block = (blocks, 1, 1, HEAD_WIDTH, token_positions)
    area = count * GROUP * token_positions * token_positions * blocks
    heads = pl.BlockSpec(head_block, lambda j: (j + first, 0, 0))
    table = pl.BlockSpec((HALF, token_positions), lambda j: (0, 0))
    return pl.pallas_call(
        backward_kernel,
        grid=(count,),
        in_specs=[
            heads,
            pl.BlockSpec(key_block, lambda j: (0, 0, j + first, 0, 0)),
            pl.BlockSpec(key_block, lambda j: (0, 1, j + first, 0, 0)),
            heads,
            heads,
            pl.BlockSpec((GROUP, 1, token_positions), lambda j: (j + first, 0, 0)),
            table,
            table,
        ],
        out_specs=[
            pl.BlockSpec(head_block, lambda j: (j, 0, 0)),
            pl.BlockSpec((blocks, 2, 1, HEAD_WIDTH, token_positions), lambda j: (0, 0, j, 0, 0)),
        ],
        out_shape=[
            jax.ShapeDtypeStruct((count * GROUP, HEAD_WIDTH, token_positions), jnp.bfloat16),
            jax.ShapeDtypeStruct(
                (blocks, 2, count, HEAD_WIDTH, token_positions), jnp.bfloat16
            ),
        ],
        compiler_params=pltpu.CompilerParams(vmem_limit_bytes=VMEM_LIMIT),
        cost_estimate=pl.CostEstimate(
            flops=40 * HEAD_WIDTH * area, bytes_accessed=10 * query.size, transcendentals=area
        ),
        name="attend_backward",
    )(query, keyval, keyval, back_mixed, mixed, lse, cosine, sine)


def move_along(value, distance):
    blocks = lax.axis_size("ctx")
    pairs = [(i, i + distance) for i in range(blocks) if 0 <= i + distance < blocks]
    return lax.ppermute(value, "ctx", pairs)


def trade(value, axis, step):
    pairs = [(i, i ^ step) for i in range(lax.axis_size(axis))]
    return lax.ppermute(value, axis, pairs)


def add_low(left, right):
    return (left.astype(jnp.float32) + right.astype(jnp.float32)).astype(jnp.bfloat16)


def scatter_sum(value, axis):
    size = lax.axis_size(axis)
    index = lax.axis_index(axis)
    rows = value.shape[0] // size
    step = 1
    while step < size:
        count = value.shape[0] // (2 * rows)
        split = value.reshape(count, 2, rows, value.shape[-1])
        second = (index // step) % 2 == 1
        kept = jnp.where(second, split[:, 1], split[:, 0])
        sent = jnp.where(second, split[:, 0], split[:, 1])
        value = add_low(kept, trade(sent, axis, step)).reshape(count * rows, value.shape[-1])
        step *= 2
    return value


def whole_sum(value, others):
    half_rows = value.shape[0] // 2
    second = lax.axis_index("ctx") % 2 == 1
    upper, lower = value[:half_rows], value[half_rows:]
    received = trade(jnp.where(second, upper, lower), "ctx", 1)
    total = add_low(jnp.where(second, lower, upper), received)
    for axis, first_step in others:
        step = first_step
        while step < lax.axis_size(axis):
            total = add_low(total, trade(total, axis, step))
            step *= 2
    received = trade(total, "ctx", 1)
    return jnp.concatenate(
        [jnp.where(second, received, total), jnp.where(second, total, received)], 0
    ).astype(jnp.float32)


def on_device(
    tokens, cotangent, input_gain, w_query, w_keyval, w_output, middle_gain, w_gate, w_up, w_down
):
    half = lax.axis_index("tp")
    low_half = half == 0
    pair = [(0, 1), (1, 0)]

    def to_partner(value_rows):
        return lax.ppermute(value_rows, "tp", pair)

    def in_order(mine, received):
        return jnp.concatenate(
            [jnp.where(low_half, mine, received), jnp.where(low_half, received, mine)], 0
        )

    def take(value_rows, index):
        return lax.dynamic_index_in_dim(value_rows, index, 0, keepdims=False)

    tokens_own = in_order(take(tokens, half), to_partner(take(tokens, 1 - half)))
    full_gain_one, full_gain_two = (
        lax.all_gather(input_gain, "fsdp", axis=0, tiled=True),
        lax.all_gather(middle_gain, "fsdp", axis=0, tiled=True),
    )
    full_in = lax.all_gather(jnp.concatenate([w_query, w_keyval], 1), "fsdp", axis=0, tiled=True)
    full_output = lax.all_gather(w_output, "fsdp", axis=0, tiled=True)
    full_gate = lax.all_gather(w_gate, "fsdp", axis=0, tiled=True)
    full_up = lax.all_gather(w_up, "fsdp", axis=0, tiled=True)
    full_down = lax.all_gather(w_down, "fsdp", axis=0, tiled=True)
    cotangent_received = to_partner(cotangent)
    cotangent_own = in_order(take(cotangent, half), take(cotangent_received, half))
    cotangent_other = in_order(take(cotangent, 1 - half), take(cotangent_received, 1 - half))

    token_positions = tokens_own.shape[0]
    cosine, sine = rope_tables(token_positions, lax.axis_index("ctx") * token_positions)
    gain_one = full_gain_one.astype(jnp.float32)
    inputs = tokens_own.astype(jnp.float32)
    unit_one, inverse_one = normalize(inputs)
    normed_one = (unit_one * gain_one).astype(jnp.bfloat16)
    keyval_raw = dot(full_in[:, QUERY_WIDTH:], normed_one, 0, 1)
    keyval_low = jnp.concatenate(
        [apply_rotary(keyval_raw[:KEY_WIDTH], cosine, sine), keyval_raw[KEY_WIDTH:]], 0
    ).astype(jnp.bfloat16)
    blocks = lax.axis_size("ctx")
    keyval = jnp.stack([keyval_low] + [move_along(keyval_low, s) for s in range(1, blocks)], 0)
    keyval = keyval.reshape(blocks, 2, KEYVAL_HEADS, HEAD_WIDTH, token_positions)
    query_raw = dot(full_in[:, :QUERY_WIDTH], normed_one, 0, 1)
    query_low = (
        apply_rotary(query_raw, cosine, sine)
        .astype(jnp.bfloat16)
        .reshape(QUERY_HEADS, HEAD_WIDTH, token_positions)
    )
    mixed_heads, lse = attend_forward(query_low, keyval)
    mixed_low = mixed_heads.reshape(QUERY_WIDTH, token_positions)
    middle = inputs + dot(mixed_low, full_output, 0, 0)

    gain_two = full_gain_two.astype(jnp.float32)
    unit_two, inverse_two = normalize(middle)
    normed_two = (unit_two * gain_two).astype(jnp.bfloat16)
    normed_other = to_partner(normed_two)

    def feed(rows, back_rows):
        gate_proj = dot(rows, full_gate, 1, 0)
        up_proj = dot(rows, full_up, 1, 0)
        sigmoid_gate = jax.nn.sigmoid(gate_proj)
        swish_gate = gate_proj * sigmoid_gate
        hidden = (swish_gate * up_proj).astype(jnp.bfloat16)
        back_hidden = dot(back_rows, full_down, 1, 0)
        back_gate = (
            back_hidden * up_proj * sigmoid_gate * (1.0 + gate_proj * (1.0 - sigmoid_gate))
        ).astype(jnp.bfloat16)
        back_up = (back_hidden * swish_gate).astype(jnp.bfloat16)
        return (hidden, back_gate, back_up)

    def feed_input_back(back_gate, back_up):
        return dot(back_gate, full_gate, 1, 1) + dot(back_up, full_up, 1, 1)

    hidden_own, back_gate_own, back_up_own = feed(normed_two, cotangent_own)
    hidden_other, back_gate_other, back_up_other = feed(normed_other, cotangent_other)
    back_two_received = to_partner(
        feed_input_back(back_gate_other, back_up_other).astype(jnp.bfloat16)
    )
    back_two = feed_input_back(back_gate_own, back_up_own) + back_two_received.astype(jnp.float32)
    feed_received = to_partner(dot(hidden_other, full_down, 1, 1).astype(jnp.bfloat16))
    result_own = (
        middle + dot(hidden_own, full_down, 1, 1) + feed_received.astype(jnp.float32)
    ).astype(jnp.bfloat16)

    def feed_gradient(left_own, right_own, left_other, right_other):
        gradient = dot(left_own, right_own, 0, 0) + dot(left_other, right_other, 0, 0)
        shared = scatter_sum(gradient.astype(jnp.bfloat16), "fsdp")
        return whole_sum(shared, (("ctx", 2),))

    share_down = feed_gradient(cotangent_own, hidden_own, cotangent_other, hidden_other)
    share_gate = feed_gradient(normed_two, back_gate_own, normed_other, back_gate_other)
    share_up = feed_gradient(normed_two, back_up_own, normed_other, back_up_other)

    grad_gain_two = jnp.sum(back_two * unit_two, axis=0)
    back_middle = cotangent_own.astype(jnp.float32) + norm_back(
        back_two * gain_two, unit_two, inverse_two
    )
    back_attention = back_middle.astype(jnp.bfloat16)
    back_mixed = dot(full_output, back_attention, 1, 1).astype(jnp.bfloat16)
    back_mixed = back_mixed.reshape(query_low.shape)
    grad_output = dot(mixed_low, back_attention, 1, 0).astype(jnp.bfloat16)
    share_output = whole_sum(scatter_sum(grad_output, "fsdp"), (("tp", 1), ("ctx", 2)))

    back_query = []
    back_key = []
    back_value = []
    for first, count in ((0, 3), (3, 2)):
        part_query, part_keyval = attend_backward(
            query_low, keyval, back_mixed, mixed_heads, lse, cosine, sine, first, count
        )
        part_keyval = part_keyval.reshape(blocks, 2 * count * HEAD_WIDTH, token_positions)
        owned = part_keyval[0].astype(jnp.float32)
        for s in range(1, blocks):
            owned += move_along(part_keyval[s], -s).astype(jnp.float32)
        back_query.append(part_query.reshape(-1, token_positions))
        back_key.append(
            apply_rotary(owned[: count * HEAD_WIDTH], cosine, -sine).astype(jnp.bfloat16)
        )
        back_value.append(owned[count * HEAD_WIDTH :].astype(jnp.bfloat16))
    back_in = jnp.concatenate(back_query + back_key + back_value, 0)
    grad_in = dot(normed_one, back_in, 0, 1)
    back_one = dot(back_in, full_in, 0, 1)
    grad_gain_one = jnp.sum(back_one * unit_one, axis=0)
    back_inputs = back_middle + norm_back(back_one * gain_one, unit_one, inverse_one)

    def to_positions(value_rows):
        split = value_rows.reshape(2, token_positions // 2, value_rows.shape[-1])
        received = to_partner(take(split, 1 - half))
        return in_order(take(split, half)[None], received[None])

    result = to_positions(result_own)
    grad_tokens = to_positions(back_inputs.astype(jnp.bfloat16)).astype(jnp.float32)
    gradients = jnp.concatenate([grad_in, grad_gain_one[:, None], grad_gain_two[:, None]], 1)
    share_in = lax.psum(
        lax.psum_scatter(
            gradients.astype(jnp.bfloat16), "fsdp", scatter_dimension=0, tiled=True
        ),
        ("ctx", "tp"),
    ).astype(jnp.float32)
    width = full_in.shape[1]
    return (
        result,
        grad_tokens,
        share_in[:, width],
        share_in[:, :QUERY_WIDTH],
        share_in[:, QUERY_WIDTH:width],
        share_output,
        share_in[:, width + 1],
        share_gate,
        share_up,
        share_down,
    )


def solution(mesh):
    rows = P("fsdp", ("ctx", "tp"), None)
    specs = (
        P("fsdp"), P("fsdp", None), P("fsdp", None), P("fsdp", None),
        P("fsdp"), P("fsdp", "tp"), P("fsdp", "tp"), P("fsdp", "tp"),
    )
    return jax.shard_map(
        on_device,
        mesh=mesh,
        in_specs=(rows, rows) + specs,
        out_specs=(rows, rows) + specs,
        check_vma=False,
    )
```
